32 devices in a mesh: child: 2 (over core), row: 4 (over y, x), col: 4 (over z).
Axes of the slice: x: 2, y: 2, z: 4, core: 2. Of those that a mesh axis runs over, the one named last changes fastest.
Arguments:
- child_fronts: float32 [2, 4096, 4096], P('child', 'row', 'col'), as said below
- root_front: float32 [8192, 8192], P('col', ('child', 'row')), as said below
- block_maps: int32 [2, 24], replicated, may hold values from 0 to 63, as said below
Outputs:
- child_factor: float32 [2, 4096, 1024], P('child', 'row')
- root_factor: float32 [8192, 512], P('col')
- root_trailing: float32 [8192, 8192], P('col', ('child', 'row'))
The draws below stay inside these ranges and needn't reach their ends.
Inputs may be any that keep to these rules, and one draw needn't show every extreme that they name: `block_maps`: row c lists 24 different root blocks in increasing order; block 0 appears in the first row and the last root block in the last row. `child_fronts`: each front is symmetric and positive definite. `root_front`: symmetric and positive definite.
All inputs are finite; a program needn't handle non-finite values.
Results may differ from the reference program's by a relative error of at most 0.0003.
Values may be sent and summed in bfloat16 or wider, within the bound.
A program may use at most 256 MiB of HBM per device.

```python
import math
import jax
import jax.numpy as jnp
from jax import lax

FC = 4096
R = 8192
PANEL = 512
CPAN = 2
RPAN = 1
BLK = 128
CHILDREN = 2
PIV = 1024
NCB = 24


def symmetric_front(key, count, order):
    base = jax.random.uniform(jax.random.fold_in(key, 11), (count, order, order), jnp.float32, -1.0, 1.0)
    mirrored = 0.5 * (base + jnp.swapaxes(base, 1, 2))
    diag_values = jax.random.uniform(jax.random.fold_in(key, 12), (count, order), jnp.float32, 1.3, 2.9) * math.sqrt(order)
    on_diag = jnp.eye(order, dtype=jnp.bool_)
    front = jnp.where(on_diag[None], diag_values[:, :, None], mirrored)
    factor_scale = 0.06 * math.sqrt(math.sqrt(order))
    loadings = jax.random.normal(jax.random.fold_in(key, 14), (count, order, 8), jnp.float32) * factor_scale
    for term_index in range(8):
        column = loadings[:, :, term_index]
        front = front + column[:, :, None] * column[:, None, :]
    return front


def draw_child_fronts(key, part):
    return symmetric_front(key, CHILDREN, FC)


def draw_root_front(key, part):
    return symmetric_front(key, 1, R)[0]


def draw_block_maps(key, part):
    block_count = R // BLK
    row_list = []
    for child_index in range(CHILDREN):
        shuffled = jax.random.permutation(jax.random.fold_in(key, child_index), block_count)
        chosen = jnp.sort(shuffled[:NCB])
        if child_index == 0:
            chosen = chosen.at[0].set(0)
        if child_index == CHILDREN - 1:
            chosen = chosen.at[NCB - 1].set(block_count - 1)
        row_list.append(chosen)
    return jnp.stack(row_list).astype(jnp.int32)


def setup_inputs(seed: int = 0) -> dict:
    keys = jax.random.split(jax.random.key(seed), 4)
    return {
        "child_fronts": draw_child_fronts(jax.random.fold_in(keys[3], 71), 0),
        "root_front": draw_root_front(jax.random.fold_in(keys[3], 71), 0),
        "block_maps": draw_block_maps(jax.random.fold_in(keys[3], 71), 0),
    }


def factor_panels(front, panel_count):
    order = front.shape[0]
    row_ids = jnp.arange(order, dtype=jnp.int32)
    columns = []
    for panel_index in range(panel_count):
        first_col = panel_index * PANEL
        diagonal = front[first_col:first_col + PANEL, first_col:first_col + PANEL]
        diag_factor = jnp.linalg.cholesky(diagonal)
        solved = lax.linalg.triangular_solve(diag_factor, front[:, first_col:first_col + PANEL], left_side=False, lower=True, transpose_a=True)
        factor_rows = jnp.where(row_ids[:, None] >= first_col, solved, 0.0)
        update_rows = jnp.where(row_ids[:, None] >= first_col + PANEL, solved, 0.0).astype(jnp.bfloat16)
        front = front - jnp.dot(update_rows.astype(jnp.float32), update_rows.T.astype(jnp.float32), preferred_element_type=jnp.float32)
        columns.append(factor_rows)
    return (front, jnp.concatenate(columns, axis=1))

def reference(child_fronts, root_front, block_maps):
    assembled = root_front
    factors = []
    offsets = jnp.arange(BLK, dtype=jnp.int32)
    for child_index in range(CHILDREN):
        trailing, factor = factor_panels(child_fronts[child_index], CPAN)
        factors.append(factor)
        targets = (block_maps[child_index][:, None] * BLK + offsets[None, :]).reshape(-1).astype(jnp.int32)
        assembled = assembled.at[targets[:, None], targets[None, :]].add(trailing[PIV:, PIV:])
    root_trailing, root_factor = factor_panels(assembled, RPAN)
    return (jnp.stack(factors), root_factor, root_trailing)
```

```python
import functools

import jax
import jax.numpy as jnp
from jax import lax
from jax.experimental import pallas as pl
from jax.experimental.pallas import tpu as pltpu
from jax.sharding import PartitionSpec as P

R = 8192
PANEL = 512
BLK = 128
PIV = 1024
NCB = 24
PB = PIV // BLK
HI = lax.Precision.HIGHEST
VMEM_LIMIT = 48 * 1024 * 1024


def small_inverse(block):
    eye = (
        lax.broadcasted_iota(jnp.int32, (BLK, BLK), 0)
        == lax.broadcasted_iota(jnp.int32, (BLK, BLK), 1)
    ).astype(jnp.float32)
    sub = lax.broadcasted_iota(jnp.int32, (8, BLK), 0)
    left = [block[8 * g : 8 * g + 8, :] for g in range(BLK // 8)]
    right = [eye[8 * g : 8 * g + 8, :] for g in range(BLK // 8)]
    for j in range(BLK):
        first, place = j // 8, j % 8
        row_left = left[first][place : place + 1, :]
        row_right = right[first][place : place + 1, :]
        scale = 1.0 / row_left[:, j : j + 1]
        row_left = row_left * scale
        row_right = row_right * scale
        for g in range(first, BLK // 8):
            column = left[g][:, j : j + 1]
            if g == first:
                if place == 7:
                    continue
                column = jnp.where(sub > place, column, 0.0)
            left[g] = left[g] - column * row_left
            right[g] = right[g] - column * row_right
    pivots = jnp.sum(jnp.concatenate(left, axis=0) * eye, axis=1, keepdims=True)
    return jnp.concatenate(right, axis=0) / jnp.sqrt(pivots)


def chol_kernel(a_ref, inv_ref, work):
    n = PANEL
    work[:, :n] = a_ref[...]
    work[:, n:] = (
        lax.broadcasted_iota(jnp.int32, (n, n), 0) == lax.broadcasted_iota(jnp.int32, (n, n), 1)
    ).astype(jnp.float32)
    ids = lax.broadcasted_iota(jnp.int32, (n, 1), 0)

    def step(k, carry):
        at = pl.multiple_of(k * BLK, BLK)
        here = pl.ds(at, BLK)
        small = small_inverse(work[here, here])
        rows = jnp.dot(small, work[here, :], precision=HI, preferred_element_type=jnp.float32)
        column = lax.dot_general(
            work[:, here], small, (((1,), (1,)), ((), ())), precision=HI,
            preferred_element_type=jnp.float32,
        )
        column = jnp.where(ids >= at + BLK, column, 0.0)
        work[...] = work[...] - jnp.dot(
            column, rows, precision=HI, preferred_element_type=jnp.float32
        )
        inv_ref[here, :] = rows[:, n:]
        return carry

    lax.fori_loop(0, n // BLK, step, 0)


def inverse_factor(diagonal):
    return pl.pallas_call(
        chol_kernel,
        out_shape=jax.ShapeDtypeStruct((PANEL, PANEL), jnp.float32),
        in_specs=[pl.BlockSpec(memory_space=pltpu.VMEM)],
        out_specs=pl.BlockSpec(memory_space=pltpu.VMEM),
        scratch_shapes=[pltpu.VMEM((PANEL, 2 * PANEL), jnp.float32)],
        compiler_params=pltpu.CompilerParams(vmem_limit_bytes=VMEM_LIMIT),
        cost_estimate=pl.CostEstimate(flops=60_000_000_000, bytes_accessed=2 << 20, transcendentals=0),
    )(diagonal)


def place_kernel(src_ref, full_ref, out_ref):
    m = pl.program_id(0) * pl.num_programs(1) + pl.program_id(1)

    @pl.when(src_ref[m] >= 0)
    def _():
        out_ref[...] = full_ref[...]

    @pl.when(src_ref[m] < 0)
    def _():
        out_ref[...] = jnp.zeros_like(out_ref)


def place(source, full, groups, width):
    _, rows, cols = full.shape
    per, inner = width // BLK, cols // BLK

    def pick(g, m, src):
        b = jnp.maximum(src[g * per + m], 0) + PB
        return (b // inner, 0, b % inner)

    return pl.pallas_call(
        place_kernel,
        grid_spec=pltpu.PrefetchScalarGridSpec(
            num_scalar_prefetch=1,
            grid=(groups, per),
            in_specs=[pl.BlockSpec((1, rows, BLK), pick)],
            out_specs=pl.BlockSpec((1, rows, BLK), lambda g, m, src: (g, 0, m)),
        ),
        out_shape=jax.ShapeDtypeStruct((groups, rows, width), full.dtype),
        compiler_params=pltpu.CompilerParams(vmem_limit_bytes=VMEM_LIMIT),
        cost_estimate=pl.CostEstimate(flops=0, bytes_accessed=48 << 20, transcendentals=0),
    )(source, full)


def column_kernel(src_ref, upd_ref, out_ref):
    c, m = pl.program_id(0), pl.program_id(1)

    @pl.when(src_ref[c, m] >= 0)
    def _():
        out_ref[...] = upd_ref[...]

    @pl.when(src_ref[c, m] < 0)
    def _():
        out_ref[...] = jnp.zeros_like(out_ref)


def column_rows(source, updates, row_count):
    _, rows, depth = updates.shape
    per = rows // BLK
    count = source.shape[1]

    def pick(c, m, src):
        a = jnp.maximum(src[c, m], 0) + PB
        return (c * row_count + a // per, a % per, 0)

    return pl.pallas_call(
        column_kernel,
        grid_spec=pltpu.PrefetchScalarGridSpec(
            num_scalar_prefetch=1,
            grid=(2, count),
            in_specs=[pl.BlockSpec((1, BLK, depth), pick)],
            out_specs=pl.BlockSpec((1, BLK, depth), lambda c, m, src: (c, m, 0)),
        ),
        out_shape=jax.ShapeDtypeStruct((2, count * BLK, depth), updates.dtype),
        compiler_params=pltpu.CompilerParams(vmem_limit_bytes=VMEM_LIMIT),
    )(source, updates)


def assemble_kernel(src_ref, root_ref, got0, got1, upd0, upd1, cols_ref, out_ref):
    q = pl.program_id(0)
    out_ref[...] = root_ref[...]
    for c, got, upd in ((0, got0, upd0), (1, got1, upd1)):
        @pl.when(src_ref[c, q] >= 0)
        def _(c=c, got=got, upd=upd):
            update = lax.dot_general(
                upd[0], cols_ref[c], (((1,), (1,)), ((), ())), preferred_element_type=jnp.float32
            )
            out_ref[...] += got[0].astype(jnp.float32) - update


def assemble(source, root, received, updates, columns, row_count):
    height, width = root.shape
    per = received.shape[1] // BLK
    depth = updates.shape[2]

    def pick(c):
        def index(q, src):
            a = jnp.maximum(src[c, q], 0) + PB
            return (c * row_count + a // per, a % per, 0)
        return index

    return pl.pallas_call(
        assemble_kernel,
        grid_spec=pltpu.PrefetchScalarGridSpec(
            num_scalar_prefetch=1,
            grid=(height // BLK,),
            in_specs=[
                pl.BlockSpec((BLK, width), lambda q, src: (q, 0)),
                pl.BlockSpec((1, BLK, width), pick(0)),
                pl.BlockSpec((1, BLK, width), pick(1)),
                pl.BlockSpec((1, BLK, depth), pick(0)),
                pl.BlockSpec((1, BLK, depth), pick(1)),
                pl.BlockSpec((2, width, depth), lambda q, src: (0, 0, 0)),
            ],
            out_specs=pl.BlockSpec((BLK, width), lambda q, src: (q, 0)),
        ),
        out_shape=jax.ShapeDtypeStruct((height, width), jnp.float32),
        compiler_params=pltpu.CompilerParams(vmem_limit_bytes=VMEM_LIMIT),
    )(source, root, received, received, updates, updates, columns)


def dot_t(left, right, precision=None):
    return lax.dot_general(
        left, right, (((1,), (1,)), ((), ())), precision=precision,
        preferred_element_type=jnp.float32,
    )


def local(child_fronts, root_front, block_maps):
    tile = child_fronts[0]
    row_block, col_block = tile.shape
    row_pos, col_pos = lax.axis_index("row"), lax.axis_index("col")
    child_pos = lax.axis_index("child")
    group_pos = lax.axis_index(("child", "row"))
    row_count = lax.axis_size("row")
    groups = lax.axis_size(("child", "row"))
    height, width = root_front.shape
    assert col_block == PIV

    hits = block_maps[:, :, None] == jnp.arange(R // BLK, dtype=jnp.int32)
    inverse = jnp.max(
        jnp.where(hits, jnp.arange(NCB, dtype=jnp.int32)[None, :, None], -1), axis=1
    )
    mine = lax.dynamic_slice_in_dim(inverse, child_pos, 1, 0)[0]
    row_source = lax.dynamic_slice_in_dim(inverse, col_pos * (height // BLK), height // BLK, 1)
    col_source = lax.dynamic_slice_in_dim(inverse, group_pos * (width // BLK), width // BLK, 1)

    if row_block >= PIV:
        corner = jnp.where(row_pos == 0, tile[:PIV], 0.0)
    else:
        corner = jnp.concatenate(
            [jnp.where(row_pos == m, tile, 0.0) for m in range(PIV // row_block)], axis=0
        )
    corner = jnp.where(col_pos == 0, corner, 0.0)
    corner = jnp.concatenate(
        [corner[:PANEL, :PANEL], corner[PANEL:, :PANEL], corner[PANEL:, PANEL:]], axis=0
    )
    corner = lax.psum(corner, ("row", "col"))
    full = lax.all_gather(tile, "col", axis=0)

    inv0 = inverse_factor(corner[:PANEL])
    low = dot_t(corner[PANEL : 2 * PANEL], inv0, HI).astype(jnp.bfloat16)
    inv1 = inverse_factor(corner[2 * PANEL :] - dot_t(low, low))

    placed = place(mine, full, groups, width)
    received = lax.all_to_all(placed, ("child", "row"), split_axis=0, concat_axis=0, tiled=True)

    panel = full[0]
    row_ids = (row_pos * row_block + jnp.arange(row_block, dtype=jnp.int32))[:, None]
    fac0 = dot_t(panel[:, :PANEL], inv0, HI)
    upd0 = jnp.where(row_ids >= PANEL, fac0, 0.0).astype(jnp.bfloat16)
    fac1 = dot_t(panel[:, PANEL:] - dot_t(upd0, low), inv1, HI)
    fac1 = jnp.where(row_ids >= PANEL, fac1, 0.0)
    upd1 = jnp.where(row_ids >= PIV, fac1, 0.0).astype(jnp.bfloat16)
    child_factor = jnp.concatenate([fac0, fac1], axis=1)[None]
    updates = lax.all_gather(jnp.concatenate([upd0, upd1], axis=1), ("child", "row"), axis=0)

    columns = column_rows(col_source, updates, row_count)
    assembled = assemble(row_source, root_front, received, updates, columns, row_count)

    if width >= PANEL:
        own = jnp.where(group_pos == 0, assembled[:, :PANEL], 0.0)
    else:
        own = jnp.concatenate(
            [jnp.where(group_pos == m, assembled, 0.0) for m in range(PANEL // width)], axis=1
        )
    diagonal = lax.psum(jnp.where(col_pos == 0, own[:PANEL], 0.0), ("child", "row", "col"))
    strip = lax.psum(jnp.where(col_pos == 0, assembled[:PANEL], 0.0), "col")
    panel_rows = lax.psum(own, ("child", "row"))
    inv = inverse_factor(diagonal)
    root_factor = dot_t(panel_rows, inv, HI)
    root_ids = (col_pos * height + jnp.arange(height, dtype=jnp.int32))[:, None]
    row_update = jnp.where(root_ids >= PANEL, root_factor, 0.0).astype(jnp.bfloat16)
    col_ids = (group_pos * width + jnp.arange(width, dtype=jnp.int32))[None, :]
    col_update = jnp.dot(inv, strip, precision=HI, preferred_element_type=jnp.float32)
    col_update = jnp.where(col_ids >= PANEL, col_update, 0.0).astype(jnp.bfloat16)
    trailing = assembled - jnp.dot(row_update, col_update, preferred_element_type=jnp.float32)
    return (child_factor, root_factor, trailing)


def solution(mesh):
    return jax.shard_map(
        local,
        mesh=mesh,
        in_specs=(P("child", "row", "col"), P("col", ("child", "row")), P()),
        out_specs=(P("child", "row", None), P("col", None), P("col", ("child", "row"))),
        check_vma=False,
    )
```

```python
import functools

import jax
import jax.numpy as jnp
from jax import lax
from jax.experimental import pallas as pl
from jax.experimental.pallas import tpu as pltpu
from jax.sharding import PartitionSpec as P

R = 8192
PANEL = 512
BLK = 128
PIV = 1024
NCB = 24
PB = PIV // BLK
HI = lax.Precision.HIGHEST
VMEM_LIMIT = 48 * 1024 * 1024


def small_inverse(block):
    eye = (
        lax.broadcasted_iota(jnp.int32, (BLK, BLK), 0)
        == lax.broadcasted_iota(jnp.int32, (BLK, BLK), 1)
    ).astype(jnp.float32)
    sub = lax.broadcasted_iota(jnp.int32, (8, BLK), 0)
    left = [block[8 * g : 8 * g + 8, :] for g in range(BLK // 8)]
    right = [eye[8 * g : 8 * g + 8, :] for g in range(BLK // 8)]
    for j in range(BLK):
        first, place = j // 8, j % 8
        row_left = left[first][place : place + 1, :]
        row_right = right[first][place : place + 1, :]
        scale = 1.0 / row_left[:, j : j + 1]
        row_left = row_left * scale
        row_right = row_right * scale
        for g in range(first, BLK // 8):
            column = left[g][:, j : j + 1]
            if g == first:
                if place == 7:
                    continue
                column = jnp.where(sub > place, column, 0.0)
            left[g] = left[g] - column * row_left
            right[g] = right[g] - column * row_right
    pivots = jnp.sum(jnp.concatenate(left, axis=0) * eye, axis=1, keepdims=True)
    return jnp.concatenate(right, axis=0) / jnp.sqrt(pivots)


def chol_kernel(a_ref, inv_ref, work):
    n = PANEL
    work[:, :n] = a_ref[...]
    work[:, n:] = (
        lax.broadcasted_iota(jnp.int32, (n, n), 0) == lax.broadcasted_iota(jnp.int32, (n, n), 1)
    ).astype(jnp.float32)
    ids = lax.broadcasted_iota(jnp.int32, (n, 1), 0)

    def step(k, carry):
        at = pl.multiple_of(k * BLK, BLK)
        here = pl.ds(at, BLK)
        small = small_inverse(work[here, here])
        rows = jnp.dot(small, work[here, :], precision=HI, preferred_element_type=jnp.float32)
        column = lax.dot_general(
            work[:, here], small, (((1,), (1,)), ((), ())), precision=HI,
            preferred_element_type=jnp.float32,
        )
        column = jnp.where(ids >= at + BLK, column, 0.0)
        work[...] = work[...] - jnp.dot(
            column, rows, precision=HI, preferred_element_type=jnp.float32
        )
        inv_ref[here, :] = rows[:, n:]
        return carry

    lax.fori_loop(0, n // BLK, step, 0)


def inverse_factor(diagonal):
    return pl.pallas_call(
        chol_kernel,
        out_shape=jax.ShapeDtypeStruct((PANEL, PANEL), jnp.float32),
        in_specs=[pl.BlockSpec(memory_space=pltpu.VMEM)],
        out_specs=pl.BlockSpec(memory_space=pltpu.VMEM),
        scratch_shapes=[pltpu.VMEM((PANEL, 2 * PANEL), jnp.float32)],
        compiler_params=pltpu.CompilerParams(vmem_limit_bytes=VMEM_LIMIT),
        cost_estimate=pl.CostEstimate(flops=1_000_000, bytes_accessed=2 << 20, transcendentals=0),
    )(diagonal)


def place_kernel(src_ref, full_ref, out_ref):
    m = pl.program_id(0) * pl.num_programs(1) + pl.program_id(1)

    @pl.when(src_ref[m] >= 0)
    def _():
        out_ref[...] = full_ref[...]

    @pl.when(src_ref[m] < 0)
    def _():
        out_ref[...] = jnp.zeros_like(out_ref)


def place(source, full, groups, width):
    _, rows, cols = full.shape
    per, inner = width // BLK, cols // BLK

    def pick(g, m, src):
        b = jnp.maximum(src[g * per + m], 0) + PB
        return (b // inner, 0, b % inner)

    return pl.pallas_call(
        place_kernel,
        grid_spec=pltpu.PrefetchScalarGridSpec(
            num_scalar_prefetch=1,
            grid=(groups, per),
            in_specs=[pl.BlockSpec((1, rows, BLK), pick)],
            out_specs=pl.BlockSpec((1, rows, BLK), lambda g, m, src: (g, 0, m)),
        ),
        out_shape=jax.ShapeDtypeStruct((groups, rows, width), full.dtype),
        compiler_params=pltpu.CompilerParams(vmem_limit_bytes=VMEM_LIMIT),
        cost_estimate=pl.CostEstimate(flops=0, bytes_accessed=48 << 20, transcendentals=0),
    )(source, full)


def column_kernel(src_ref, upd_ref, out_ref):
    c, m = pl.program_id(0), pl.program_id(1)

    @pl.when(src_ref[c, m] >= 0)
    def _():
        out_ref[...] = upd_ref[...]

    @pl.when(src_ref[c, m] < 0)
    def _():
        out_ref[...] = jnp.zeros_like(out_ref)


def column_rows(source, updates, row_count):
    _, rows, depth = updates.shape
    per = rows // BLK
    count = source.shape[1]

    def pick(c, m, src):
        a = jnp.maximum(src[c, m], 0) + PB
        return (c * row_count + a // per, a % per, 0)

    return pl.pallas_call(
        column_kernel,
        grid_spec=pltpu.PrefetchScalarGridSpec(
            num_scalar_prefetch=1,
            grid=(2, count),
            in_specs=[pl.BlockSpec((1, BLK, depth), pick)],
            out_specs=pl.BlockSpec((1, BLK, depth), lambda c, m, src: (c, m, 0)),
        ),
        out_shape=jax.ShapeDtypeStruct((2, count * BLK, depth), updates.dtype),
        compiler_params=pltpu.CompilerParams(vmem_limit_bytes=VMEM_LIMIT),
    )(source, updates)


def assemble_kernel(src_ref, root_ref, got0, got1, upd0, upd1, cols_ref, out_ref):
    q = pl.program_id(0)
    out_ref[...] = root_ref[...]
    for c, got, upd in ((0, got0, upd0), (1, got1, upd1)):
        @pl.when(src_ref[c, q] >= 0)
        def _(c=c, got=got, upd=upd):
            update = lax.dot_general(
                upd[0], cols_ref[c], (((1,), (1,)), ((), ())), preferred_element_type=jnp.float32
            )
            out_ref[...] += got[0] - update


def assemble(source, root, received, updates, columns, row_count):
    height, width = root.shape
    per = received.shape[1] // BLK
    depth = updates.shape[2]

    def pick(c):
        def index(q, src):
            a = jnp.maximum(src[c, q], 0) + PB
            return (c * row_count + a // per, a % per, 0)
        return index

    return pl.pallas_call(
        assemble_kernel,
        grid_spec=pltpu.PrefetchScalarGridSpec(
            num_scalar_prefetch=1,
            grid=(height // BLK,),
            in_specs=[
                pl.BlockSpec((BLK, width), lambda q, src: (q, 0)),
                pl.BlockSpec((1, BLK, width), pick(0)),
                pl.BlockSpec((1, BLK, width), pick(1)),
                pl.BlockSpec((1, BLK, depth), pick(0)),
                pl.BlockSpec((1, BLK, depth), pick(1)),
                pl.BlockSpec((2, width, depth), lambda q, src: (0, 0, 0)),
            ],
            out_specs=pl.BlockSpec((BLK, width), lambda q, src: (q, 0)),
        ),
        out_shape=jax.ShapeDtypeStruct((height, width), jnp.float32),
        compiler_params=pltpu.CompilerParams(vmem_limit_bytes=VMEM_LIMIT),
    )(source, root, received, received, updates, updates, columns)


def dot_t(left, right, precision=None):
    return lax.dot_general(
        left, right, (((1,), (1,)), ((), ())), precision=precision,
        preferred_element_type=jnp.float32,
    )


def spread(block, col_pos, parts=4):
    count = lax.axis_size("col")
    pieces = []
    for piece in jnp.split(block, parts, axis=0):
        for hop in range(count - 1):
            arrived = lax.ppermute(piece, "col", [(hop, hop + 1)])
            piece = jnp.where(col_pos == hop + 1, arrived, piece)
        pieces.append(piece)
    return jnp.concatenate(pieces, axis=0)


def local(child_fronts, root_front, block_maps):
    tile = child_fronts[0]
    row_block, col_block = tile.shape
    row_pos, col_pos = lax.axis_index("row"), lax.axis_index("col")
    child_pos = lax.axis_index("child")
    group_pos = lax.axis_index(("child", "row"))
    row_count = lax.axis_size("row")
    groups = lax.axis_size(("child", "row"))
    height, width = root_front.shape
    assert col_block == PIV

    hits = block_maps[:, :, None] == jnp.arange(R // BLK, dtype=jnp.int32)
    inverse = jnp.max(
        jnp.where(hits, jnp.arange(NCB, dtype=jnp.int32)[None, :, None], -1), axis=1
    )
    mine = lax.dynamic_slice_in_dim(inverse, child_pos, 1, 0)[0]
    row_source = lax.dynamic_slice_in_dim(inverse, col_pos * (height // BLK), height // BLK, 1)
    col_source = lax.dynamic_slice_in_dim(inverse, group_pos * (width // BLK), width // BLK, 1)

    if row_block >= PIV:
        corner = jnp.where(row_pos == 0, tile[:PIV], 0.0)
    else:
        corner = jnp.concatenate(
            [jnp.where(row_pos == m, tile, 0.0) for m in range(PIV // row_block)], axis=0
        )
    corner = jnp.where(col_pos == 0, corner, 0.0)
    corner = jnp.concatenate(
        [corner[:PANEL, :PANEL], corner[PANEL:, :PANEL], corner[PANEL:, PANEL:]], axis=0
    )
    corner = lax.psum(corner, ("row", "col"))
    full = lax.all_gather(tile, "col", axis=0)

    largest = lax.pmax(jnp.max(jnp.abs(tile)), ("child", "row", "col"))
    unscale = jnp.maximum(largest, 1e-30).reshape(1) * (1.0 / 32768.0)
    placed = (place(mine, full, groups, width) * (1.0 / unscale)).astype(jnp.float16)
    corner, placed = lax.optimization_barrier((corner, placed))

    inv0 = inverse_factor(corner[:PANEL])
    low = dot_t(corner[PANEL : 2 * PANEL], inv0, HI).astype(jnp.bfloat16)
    inv1 = inverse_factor(corner[2 * PANEL :] - dot_t(low, low))

    received = lax.all_to_all(placed, ("child", "row"), split_axis=0, concat_axis=0, tiled=True)
    received = received.astype(jnp.float32) * unscale

    panel = full[0]
    row_ids = (row_pos * row_block + jnp.arange(row_block, dtype=jnp.int32))[:, None]
    fac0 = dot_t(panel[:, :PANEL], inv0, HI)
    upd0 = jnp.where(row_ids >= PANEL, fac0, 0.0).astype(jnp.bfloat16)
    fac1 = dot_t(panel[:, PANEL:] - dot_t(upd0, low), inv1, HI)
    fac1 = jnp.where(row_ids >= PANEL, fac1, 0.0)
    upd1 = jnp.where(row_ids >= PIV, fac1, 0.0).astype(jnp.bfloat16)
    child_factor = jnp.concatenate([fac0, fac1], axis=1)[None]
    updates = lax.all_gather(jnp.concatenate([upd0, upd1], axis=1), ("child", "row"), axis=0)

    columns = column_rows(col_source, updates, row_count)
    assembled = assemble(row_source, root_front, received, updates, columns, row_count)

    if width >= PANEL:
        own = jnp.where(group_pos == 0, assembled[:, :PANEL], 0.0)
    else:
        own = jnp.concatenate(
            [jnp.where(group_pos == m, assembled, 0.0) for m in range(PANEL // width)], axis=1
        )
    diagonal = lax.psum(jnp.where(col_pos == 0, own[:PANEL], 0.0), ("child", "row", "col"))
    strip = spread(assembled[:PANEL], col_pos)
    panel_rows = lax.psum(own, ("child", "row"))
    inv = inverse_factor(diagonal)
    root_factor = dot_t(panel_rows, inv, HI)
    root_ids = (col_pos * height + jnp.arange(height, dtype=jnp.int32))[:, None]
    row_update = jnp.where(root_ids >= PANEL, root_factor, 0.0).astype(jnp.bfloat16)
    col_ids = (group_pos * width + jnp.arange(width, dtype=jnp.int32))[None, :]
    col_update = jnp.dot(inv, strip, precision=HI, preferred_element_type=jnp.float32)
    col_update = jnp.where(col_ids >= PANEL, col_update, 0.0).astype(jnp.bfloat16)
    trailing = assembled - jnp.dot(row_update, col_update, preferred_element_type=jnp.float32)
    return (child_factor, root_factor, trailing)


def solution(mesh):
    return jax.shard_map(
        local,
        mesh=mesh,
        in_specs=(P("child", "row", "col"), P("col", ("child", "row")), P()),
        out_specs=(P("child", "row", None), P("col", None), P("col", ("child", "row"))),
        check_vma=False,
    )
```
